256 devices in a mesh: ctx: 64 (over y_lo, z, x), head: 4 (over y_hi, core).
Axes of the slice: x: 4, y: 4 (y_hi: 2, y_lo: 2; y = y_hi * 2 + y_lo), z: 8, core: 2. Of those that a mesh axis runs over, the one named last changes fastest.
Arguments:
- queries: bfloat16 [32768, 2048], P('ctx', 'head'), may hold values from -30 to 30
- key_rows: bfloat16 [32768, 2048], P('ctx', 'head'), may hold values from -6 to 6
- value_rows: bfloat16 [32768, 2048], P('ctx', 'head'), may hold values from -6 to 6
Outputs:
- attended: bfloat16 [32768, 2048], P(('ctx', 'head'))
The draws below stay inside these ranges and needn't reach their ends.
All inputs are finite; a program needn't handle non-finite values.
Results may differ from the reference program's by a relative error of at most 0.0041.
Values may be sent and summed in bfloat16 or wider, within the bound.
A program may use at most 128 MiB of HBM per device.

```python
import jax
import jax.numpy as jnp
from jax import lax

HEADS = 16
HD = 128
WINDOW = 1024
STRIDE = 2048
SUMM = 16
TOK_DEV = 512
TOKENS = 32768


def draw_key_rows(key, part):
    key = jax.random.fold_in(key, 11)
    feat_width = HEADS * HD
    result = jnp.clip(jax.random.normal(key, (TOKENS, feat_width), jnp.float32), -6.0, 6.0)
    return result.astype(jnp.bfloat16)


def draw_queries(key, part):
    key = jax.random.fold_in(key, 12)
    feat_width = HEADS * HD
    result = jnp.clip(1.5 * jax.random.normal(key, (TOKENS, feat_width), jnp.float32), -9.0, 9.0)
    return result.astype(jnp.bfloat16)


def level_of(stream_key, shape, shards, low, largest):
    loudness = 1.0
    for dim, parts in shards:
        draws = jax.random.uniform(jax.random.fold_in(jax.random.fold_in(stream_key, 6), dim), (parts,), jnp.float32, low / len(shards), largest / len(shards))
        loudness = loudness * jnp.repeat(jnp.exp(draws), shape[dim] // parts).reshape((-1,) + (1,) * (len(shape) - 1 - dim))
    return loudness


def noise(stream_key, extent, width, most, shards=(), kind=jnp.bfloat16):
    values = width * jax.random.normal(stream_key, extent, jnp.float32)
    if shards:
        values = values * level_of(stream_key, extent, shards, -0.22, 0.18)
    return jnp.clip(values, -most, most).astype(kind)


def setup_inputs(seed: int = 0) -> dict:
    keys = jax.random.split(jax.random.key(seed), 4)
    queries = draw_queries(jax.random.fold_in(keys[3], 71), 0)
    key_rows = draw_key_rows(jax.random.fold_in(keys[3], 71), 0)
    value_rows = noise(keys[2], (TOKENS, HEADS * HD), 1.0, 6.0, ((0, 64), (1, 4)))
    return {"queries": queries, "key_rows": key_rows, "value_rows": value_rows}


def reference(queries, key_rows, value_rows):
    feat_width = HEADS * HD
    score_scale = HD ** -0.5
    blk_rows = min(512, TOK_DEV)
    blk_count = TOKENS // blk_rows
    padding = jnp.zeros((WINDOW, feat_width), key_rows.dtype)
    keys_ext = jnp.concatenate([padding, key_rows], axis=0)
    values_ext = jnp.concatenate([padding, value_rows], axis=0)
    groups = TOKENS // STRIDE
    summ_keys = key_rows.reshape(groups, STRIDE, feat_width)[:, STRIDE - SUMM:].reshape(groups * SUMM, HEADS, HD).astype(jnp.float32)
    summ_values = value_rows.reshape(groups, STRIDE, feat_width)[:, STRIDE - SUMM:].reshape(groups * SUMM, HEADS, HD).astype(jnp.float32)
    summ_pos = (jnp.arange(groups, dtype=jnp.int32)[:, None] * STRIDE + (STRIDE - SUMM) + jnp.arange(SUMM, dtype=jnp.int32)[None, :]).reshape(-1)

    def one_block(blk_index):
        row_start = (blk_index * blk_rows).astype(jnp.int32)
        query_blk = lax.dynamic_slice_in_dim(queries, row_start, blk_rows, 0).reshape(blk_rows, HEADS, HD).astype(jnp.float32)
        key_slab = lax.dynamic_slice_in_dim(keys_ext, row_start, blk_rows + WINDOW, 0).reshape(blk_rows + WINDOW, HEADS, HD).astype(jnp.float32)
        value_slab = lax.dynamic_slice_in_dim(values_ext, row_start, blk_rows + WINDOW, 0).reshape(blk_rows + WINDOW, HEADS, HD).astype(jnp.float32)
        query_pos = row_start + jnp.arange(blk_rows, dtype=jnp.int32)
        key_pos = row_start - WINDOW + jnp.arange(blk_rows + WINDOW, dtype=jnp.int32)
        near_mask = (key_pos[None, :] <= query_pos[:, None]) & (query_pos[:, None] - key_pos[None, :] < WINDOW) & (key_pos[None, :] >= 0)
        far_mask = summ_pos[None, :] <= query_pos[:, None] - WINDOW
        near_scores = jnp.einsum('qhd,khd->hqk', query_blk, key_slab) * score_scale
        near_scores = jnp.where(near_mask[None], near_scores, -jnp.inf)
        far_scores = jnp.einsum('qhd,khd->hqk', query_blk, summ_keys) * score_scale
        far_scores = jnp.where(far_mask[None], far_scores, -jnp.inf)
        row_max = jnp.maximum(jnp.max(near_scores, axis=-1), jnp.max(far_scores, axis=-1))
        near_weights = jnp.exp(near_scores - row_max[..., None])
        far_weights = jnp.exp(far_scores - row_max[..., None])
        weight_sum = jnp.sum(near_weights, axis=-1) + jnp.sum(far_weights, axis=-1)
        near_round = lax.optimization_barrier(near_weights.astype(jnp.bfloat16)).astype(jnp.float32)
        far_round = lax.optimization_barrier(far_weights.astype(jnp.bfloat16)).astype(jnp.float32)
        mixed = jnp.einsum('hqk,khd->qhd', near_round, value_slab) + jnp.einsum('hqk,khd->qhd', far_round, summ_values)
        return (mixed / jnp.transpose(weight_sum)[:, :, None]).astype(jnp.bfloat16).reshape(blk_rows, feat_width)

    blocks_out = lax.map(one_block, jnp.arange(blk_count, dtype=jnp.int32))
    return blocks_out.reshape(TOKENS, feat_width)
```

```python
import jax
import jax.numpy as jnp
from jax import lax
from jax.experimental import pallas as pl
from jax.experimental.pallas import tpu as pltpu
from jax.sharding import PartitionSpec as P

HD = 128
BLK = 512
RING = 4
HEAD_DEV = 4
ROWS = RING * BLK
WINDOW = 1024
SUMM = 16
GROUPS = 16
FAR = GROUPS * SUMM
TILE = 128
BAND = WINDOW + TILE
STEPS = ROWS // TILE
PIECES = 4
PIECE = BLK // PIECES
PEERS = (1, 3, 2)
LOW = -1e30
EXP_SCALE = HD**-0.5 * 1.4426950408889634
MESH = pl.DeviceIdType.MESH


def kernel(
    q_in, k_in, v_in, out, stage, q_all, kv, far, o_all, bias,
    stage_sem, kv_sem, q_sem, halo_sem, far_sem, o_sem, send_sem, halo_send, far_send, o_send,
):
    ctx, h = lax.axis_index("ctx"), lax.axis_index("head")
    x, group = lax.rem(ctx, RING), ctx // RING
    first = ctx - x

    def ring(dx):
        return lax.rem(x + dx + RING, RING)

    def group_peer(d):
        return (lax.rem(ctx + RING * d, RING * GROUPS), h)

    def cols(place):
        return pl.ds(pl.multiple_of(place * HD, HD), HD)

    def rows(start, size):
        return pl.ds(pl.multiple_of(start, TILE), size)

    def wait(ref, sem):
        pltpu.make_async_copy(ref, ref, sem).wait()

    def piece_of(dr):
        return lax.rem(h + dr, HEAD_DEV)

    staging = [
        pltpu.make_async_copy(src, stage.at[i], stage_sem.at[i])
        for i, src in ((0, k_in), (1, v_in), (2, q_in))
    ]
    for copy in staging:
        copy.start()

    barrier = pltpu.get_barrier_semaphore()
    partners = 0
    for dx in range(RING):
        for dh in range(HEAD_DEV):
            if dx or dh:
                pl.semaphore_signal(
                    barrier, inc=1, device_id=(first + ring(dx), lax.rem(h + dh, HEAD_DEV)),
                    device_id_type=MESH,
                )
                partners += 1
    for d in range(1, GROUPS):
        pl.semaphore_signal(barrier, inc=1, device_id=group_peer(d), device_id_type=MESH)
        partners += 1

    col = lax.broadcasted_iota(jnp.int32, (TILE, FAR), 1)
    row = lax.broadcasted_iota(jnp.int32, (TILE, FAR), 0)
    known = (col >= SUMM) & (col < SUMM * (group + 1))
    for case in range(3):
        seen = known
        if case == 0:
            seen = known & (col >= 2 * SUMM)
        if case == 1:
            seen = known & ((col >= 2 * SUMM) | (col - SUMM <= row - (TILE - SUMM)))
        bias[case] = jnp.where(seen, 0.0, LOW)
    far[:, 0:SUMM, :] = jnp.zeros((2, SUMM, HD), jnp.bfloat16)

    pl.semaphore_wait(barrier, partners)

    for copy in staging:
        copy.wait()
    own_kv = rows(WINDOW + x * BLK, BLK)
    pltpu.make_async_copy(stage.at[pl.ds(0, 2), :, cols(x)], kv.at[:, own_kv], kv_sem.at[x, 0]).start()
    for p in range(PIECES):
        for dx in PEERS:
            place = ring(dx)
            span = pl.ds(p * PIECE, PIECE)
            pltpu.make_async_remote_copy(
                src_ref=stage.at[pl.ds(0, 2), span, cols(place)],
                dst_ref=kv.at[:, rows(WINDOW + x * BLK + p * PIECE, PIECE)],
                send_sem=send_sem.at[0],
                recv_sem=kv_sem.at[x, p],
                device_id=(first + place, h),
                device_id_type=MESH,
            ).start()
    for dr in range(PIECES):
        r = piece_of(dr)
        span = rows(r * PIECE, PIECE)
        pltpu.make_async_copy(
            stage.at[2, span, cols(x)], q_all.at[rows(x * BLK + r * PIECE, PIECE)], q_sem.at[0, dr]
        ).start()
        for dx in PEERS:
            place = ring(dx)
            pltpu.make_async_remote_copy(
                src_ref=stage.at[2, span, cols(place)],
                dst_ref=q_all.at[rows(x * BLK + r * PIECE, PIECE)],
                send_sem=send_sem.at[1],
                recv_sem=q_sem.at[dx, dr],
                device_id=(first + place, h),
                device_id_type=MESH,
            ).start()

    def arrived(j, p):
        wait(kv.at[:, pl.ds(0, PIECE)], kv_sem.at[j, p])

    @pl.when(x >= 2)
    def _():
        wait(kv.at[:, pl.ds(0, BLK)], kv_sem.at[x, 0])

    for p in range(PIECES):
        for j in (2, 3):
            @pl.when(x != j)
            def _():
                arrived(j, p)

            pltpu.make_async_remote_copy(
                src_ref=kv.at[:, pl.ds(WINDOW + j * BLK + p * PIECE, PIECE)],
                dst_ref=kv.at[:, pl.ds((j - 2) * BLK + p * PIECE, PIECE)],
                send_sem=halo_send,
                recv_sem=halo_sem,
                device_id=group_peer(1),
                device_id_type=MESH,
            ).start()
    for d in range(1, GROUPS):
        pltpu.make_async_remote_copy(
            src_ref=kv.at[:, pl.ds(WINDOW + ROWS - SUMM, SUMM)],
            dst_ref=far.at[:, pl.ds(d * SUMM, SUMM)],
            send_sem=far_send,
            recv_sem=far_sem,
            device_id=group_peer(d),
            device_id_type=MESH,
        ).start()

    @pl.when(x < 2)
    def _():
        wait(kv.at[:, pl.ds(0, BLK)], kv_sem.at[x, 0])

    for p in range(PIECES):
        for j in (0, 1):
            @pl.when(x != j)
            def _():
                arrived(j, p)

    wait(kv.at[:, pl.ds(0, WINDOW)], halo_sem)
    wait(far.at[:, pl.ds(SUMM, FAR - SUMM)], far_sem)

    def step(s, carry):
        u = jnp.maximum(s - HEAD_DEV, 0)
        i = lax.rem(u, 3)
        other = jnp.where(i == 0, 1, jnp.where(i == 1, 3, 2))
        dx = jnp.where(s < HEAD_DEV, 0, other)
        dr = jnp.where(s < HEAD_DEV, s, u // 3)
        j = ring(-dx)
        r = piece_of(dr)
        t = j * PIECES + r
        here = rows(t * TILE, TILE)
        wait(q_all.at[pl.ds(0, PIECE)], q_sem.at[dx, dr])
        q = q_all[here, :]
        nt = (((1,), (1,)), ((), ()))
        near = rows(t * TILE, BAND)
        s_near = lax.dot_general(q, kv[0, near, :], nt, preferred_element_type=jnp.float32)
        s_far = lax.dot_general(q, far[0], nt, preferred_element_type=jnp.float32)
        col = lax.broadcasted_iota(jnp.int32, (TILE, BAND), 1)
        row = lax.broadcasted_iota(jnp.int32, (TILE, BAND), 0)
        start = jnp.where(group == 0, jnp.maximum(WINDOW - t * TILE, 0), 0)
        admitted = (col > row) & (col <= row + WINDOW) & (col >= start)
        s_near = jnp.where(admitted, s_near, LOW)
        case = jnp.where(t < 7, 0, jnp.where(t == 7, 1, 2))
        s_far = s_far + bias[case]
        top = jnp.maximum(
            jnp.max(s_near, axis=1, keepdims=True), jnp.max(s_far, axis=1, keepdims=True)
        )
        w_near = jnp.exp2((s_near - top) * EXP_SCALE)
        w_far = jnp.exp2((s_far - top) * EXP_SCALE)
        total = jnp.sum(w_near, axis=1, keepdims=True) + jnp.sum(w_far, axis=1, keepdims=True)
        mixed = jnp.dot(w_near.astype(jnp.bfloat16), kv[1, near, :], preferred_element_type=jnp.float32)
        mixed = mixed + jnp.dot(w_far.astype(jnp.bfloat16), far[1], preferred_element_type=jnp.float32)
        o_all[here, :] = (mixed / total).astype(jnp.bfloat16)
        target = out.at[:, cols(h * RING + x)]

        @pl.when(s == 0)
        def _():
            pltpu.make_async_copy(o_all.at[here], target, o_sem).start()

        @pl.when(s > 0)
        def _():
            pltpu.make_async_remote_copy(
                src_ref=o_all.at[here],
                dst_ref=target,
                send_sem=o_send,
                recv_sem=o_sem,
                device_id=(first + j, r),
                device_id_type=MESH,
            ).start()

        return carry

    lax.fori_loop(0, STEPS, step, 0)

    wait(kv.at[:, pl.ds(0, 3 * BLK)], send_sem.at[0])
    wait(q_all.at[pl.ds(0, 3 * BLK)], send_sem.at[1])
    wait(kv.at[:, pl.ds(0, WINDOW)], halo_send)
    wait(far.at[:, pl.ds(SUMM, FAR - SUMM)], far_send)
    wait(o_all.at[pl.ds(0, ROWS - TILE)], o_send)
    wait(out, o_sem)


def on_device(queries, key_rows, value_rows):
    dma = pltpu.SemaphoreType.DMA
    return pl.pallas_call(
        kernel,
        name="attention",
        out_shape=jax.ShapeDtypeStruct((BLK // HEAD_DEV, HEAD_DEV * RING * HD), jnp.bfloat16),
        in_specs=[pl.BlockSpec(memory_space=pltpu.MemorySpace.HBM)] * 3,
        out_specs=pl.BlockSpec(memory_space=pltpu.VMEM),
        scratch_shapes=[
            pltpu.VMEM((3, BLK, RING * HD), jnp.bfloat16),
            pltpu.VMEM((ROWS, HD), jnp.bfloat16),
            pltpu.VMEM((2, WINDOW + ROWS, HD), jnp.bfloat16),
            pltpu.VMEM((2, FAR, HD), jnp.bfloat16),
            pltpu.VMEM((ROWS, HD), jnp.bfloat16),
            pltpu.VMEM((3, TILE, FAR), jnp.float32),
            dma((3,)),
            dma((RING, PIECES)),
            dma((RING, PIECES)),
            dma,
            dma,
            dma,
            dma((2,)),
            dma,
            dma,
            dma,
        ],
        compiler_params=pltpu.CompilerParams(
            collective_id=1, has_side_effects=True, vmem_limit_bytes=60 << 20
        ),
    )(queries, key_rows, value_rows)


def solution(mesh):
    placed = (P("ctx", "head"), P("ctx", "head"), P("ctx", "head"))
    return jax.shard_map(
        on_device, mesh=mesh, in_specs=placed, out_specs=P(("ctx", "head"), None), check_vma=False
    )
```

```python
import functools

import jax
import jax.numpy as jnp
from jax import lax
from jax.experimental import pallas as pl
from jax.experimental.pallas import tpu as pltpu
from jax.sharding import PartitionSpec as P

HD = 128
BLK = 512
RING = 4
HEAD_DEV = 4
ROWS = RING * BLK
WINDOW = 1024
SUMM = 16
GROUPS = 16
FAR_STEP = 0
FAR = GROUPS * SUMM
TILE = 256
BAND = WINDOW + TILE
STEPS = ROWS // TILE
HALF = BLK // TILE
PIECES = 4
PIECE = BLK // PIECES
PEERS = (1, 3, 2)
ORDER = (3, 2, 1, 0)
LOW = -1e30
EXP_SCALE = HD**-0.5 * 1.4426950408889634
MESH = pl.DeviceIdType.MESH


def kernel(
    q_in, k_in, v_in, out, q_all, kv, far, o_all, bias,
    kv_sem, q_sem, halo_sem, far_sem, o_sem, send_sem, halo_send, far_send, o_send,
    halo_ready, far_ready,
):
    ctx, h = lax.axis_index("ctx"), lax.axis_index("head")
    x, group = lax.rem(ctx, RING), ctx // RING
    first = ctx - x

    def ring(dx):
        return lax.rem(x + dx + RING, RING)

    layers = GROUPS // 2
    depth = lax.rem(group, layers)
    rank = 2 * depth + group // layers

    def ranked(place):
        return ((lax.rem(place, 2) * layers + place // 2) * RING + x, h)

    def group_peer(d):
        return (lax.rem(ctx + RING * d, RING * GROUPS), h)

    def cols(place):
        return pl.ds(pl.multiple_of(place * HD, HD), HD)

    def rows(start, size):
        return pl.ds(pl.multiple_of(start, PIECE), size)

    def wait(ref, sem):
        pltpu.make_async_copy(ref, ref, sem).wait()

    def half_of(d):
        return lax.rem(h // 2 + d, HALF)

    sources = ((0, k_in), (1, v_in))
    own = pl.ds(pl.multiple_of(WINDOW + x * BLK, BLK), BLK)
    for i, src in sources:
        pltpu.make_async_copy(src.at[:, cols(x)], kv.at[i, own], kv_sem.at[x, 0]).start()
    pltpu.make_async_copy(
        q_in.at[:, cols(x)], q_all.at[pl.ds(pl.multiple_of(x * BLK, BLK), BLK)], q_sem.at[0, 0]
    ).start()

    far[...] = jnp.zeros_like(far)

    @pl.when(group == 0)
    def _():
        kv[:, 0:WINDOW, :] = jnp.zeros((2, WINDOW, HD), jnp.bfloat16)

    barrier = pltpu.get_barrier_semaphore()
    partners = 0
    for dx in range(RING):
        for dh in range(HEAD_DEV):
            if dx or dh:
                pl.semaphore_signal(
                    barrier, inc=1, device_id=(first + ring(dx), lax.rem(h + dh, HEAD_DEV)),
                    device_id_type=MESH,
                )
                partners += 1
    for e in range(1, GROUPS):
        @pl.when(rank + e < GROUPS)
        def _():
            pl.semaphore_signal(barrier, inc=1, device_id=ranked(rank + e), device_id_type=MESH)

    col = lax.broadcasted_iota(jnp.int32, (TILE, FAR), 1)
    row = lax.broadcasted_iota(jnp.int32, (TILE, FAR), 0)
    known = (col >= SUMM) & (col < SUMM * (group + 1))
    for case in range(3):
        seen = known
        if case == 0:
            seen = known & (col >= 2 * SUMM)
        if case == 1:
            seen = known & ((col >= 2 * SUMM) | (col - SUMM <= row - (TILE - SUMM)))
        bias[case] = jnp.where(seen, 0.0, LOW)

    pl.semaphore_wait(barrier, partners + rank)
    for e in range(1, GROUPS):
        place = jnp.maximum(rank - e, 0)
        source = lax.rem(place, 2) * layers + place // 2

        @pl.when((e <= rank) & (source < group - 1))
        def _():
            pl.semaphore_signal(far_ready, inc=1, device_id=ranked(place), device_id_type=MESH)

        @pl.when((e <= rank) & (source == group - 1))
        def _():
            pl.semaphore_signal(halo_ready, inc=1, device_id=ranked(place), device_id_type=MESH)


    def send_kv(p):
        for dx in PEERS:
            place = ring(dx)
            for i, src in sources:
                pltpu.make_async_remote_copy(
                    src_ref=src.at[pl.ds(p * PIECE, PIECE), cols(place)],
                    dst_ref=kv.at[i, rows(WINDOW + x * BLK + p * PIECE, PIECE)],
                    send_sem=send_sem.at[0],
                    recv_sem=kv_sem.at[x, p],
                    device_id=(first + place, h),
                    device_id_type=MESH,
                ).start()

    def send_q(d):
        half = half_of(d)
        for dx in PEERS:
            place = ring(dx)
            pltpu.make_async_remote_copy(
                src_ref=q_in.at[rows(half * TILE, TILE), cols(place)],
                dst_ref=q_all.at[rows(x * BLK + half * TILE, TILE)],
                send_sem=send_sem.at[1],
                recv_sem=q_sem.at[dx, d],
                device_id=(first + place, h),
                device_id_type=MESH,
            ).start()

    rounds = [functools.partial(send_kv, p) for p in ORDER]
    rounds += [functools.partial(send_q, d) for d in range(HALF)]
    ahead = 2
    for send in rounds[:ahead]:
        send()

    def to_next(j, p):
        return pltpu.make_async_remote_copy(
            src_ref=kv.at[:, pl.ds(WINDOW + j * BLK + p * PIECE, PIECE)],
            dst_ref=kv.at[:, pl.ds((j - 2) * BLK + p * PIECE, PIECE)],
            send_sem=halo_send,
            recv_sem=halo_sem,
            device_id=group_peer(1),
            device_id_type=MESH,
        )

    def summary(d):
        return pltpu.make_async_remote_copy(
            src_ref=kv.at[:, pl.ds(WINDOW + ROWS - SUMM, SUMM)],
            dst_ref=far.at[:, pl.ds(d * SUMM, SUMM)],
            send_sem=far_send.at[d],
            recv_sem=far_sem.at[d],
            device_id=group_peer(d),
            device_id_type=MESH,
        )

    def arrived(j, p):
        wait(kv.at[:, pl.ds(0, PIECE)], kv_sem.at[j, p])

    @pl.when(x >= 2)
    def _():
        wait(kv.at[:, pl.ds(0, BLK)], kv_sem.at[x, 0])

    has_next = group < GROUPS - 1
    for step, p in enumerate(ORDER):
        for j in (3, 2):
            @pl.when(x != j)
            def _():
                arrived(j, p)

            if (step, j) == (0, 3):
                @pl.when(depth < layers - 1)
                def _():
                    pl.semaphore_wait(halo_ready, 1)

            @pl.when(has_next)
            def _():
                to_next(j, p).start()

        if step == FAR_STEP:
            later = jnp.where(group < layers, GROUPS - 1 - 2 * depth, layers - 1 - depth)

            ready = later - jnp.where(depth < layers - 1, 1, 0)

            @pl.when(ready > 0)
            def _():
                pl.semaphore_wait(far_ready, ready)

            for d in range(1, GROUPS):
                pl.when(group + d < GROUPS)(summary(d).start)
        if ahead + step < len(rounds):
            rounds[ahead + step]()
    for send in rounds[ahead + PIECES:]:
        send()
    wait(q_all.at[pl.ds(0, BLK)], q_sem.at[0, 0])

    @pl.when(x < 2)
    def _():
        wait(kv.at[:, pl.ds(0, BLK)], kv_sem.at[x, 0])

    for p in ORDER:
        for j in (0, 1):
            @pl.when(x != j)
            def _():
                arrived(j, p)

    for d in range(1, GROUPS):
        pl.when(d <= group)(functools.partial(wait, far.at[:, pl.ds(d * SUMM, SUMM)], far_sem.at[d]))

    def step(s, carry):
        u = jnp.maximum(s - 2, 0)
        i = lax.rem(u, 3)
        late_j = jnp.where(s < 2, x, jnp.where(i == 0, 5 - x, i - 1))
        late_d = jnp.where(s < 2, s, u // 3)
        i = jnp.maximum(s - 5, 0)
        early_j = jnp.where(
            s < 2, 2 + s, jnp.where(s < 4, x, jnp.where((s == 4) | (i == 2), 1 - x, 2 + i))
        )
        early_d = jnp.where((s < 2) | (s == 4), 0, jnp.where(s < 4, s - 2, 1))
        j = jnp.where(x >= 2, late_j, early_j)
        d = jnp.where(x >= 2, late_d, early_d)
        dx = lax.rem(x - j + RING, RING)
        half = half_of(d)
        t = j * HALF + half
        here = rows(t * TILE, TILE)

        @pl.when((s == jnp.where(x >= 2, 3, 2)) & (group > 0))
        def _():
            wait(kv.at[:, pl.ds(0, WINDOW)], halo_sem)

        @pl.when(dx > 0)
        def _():
            wait(q_all.at[pl.ds(0, TILE)], q_sem.at[dx, d])

        case = jnp.where(t < 3, 0, jnp.where(t == 3, 1, 2))
        outside = jnp.where(group == 0, WINDOW - t * TILE, 0)

        def attend(whole):
            q = q_all[here, :]
            nt = (((1,), (1,)), ((), ()))
            near = rows(t * TILE, BAND)
            scores = lax.dot_general(q, kv[0, near, :], nt, preferred_element_type=jnp.float32)
            s_far = lax.dot_general(q, far[0], nt, preferred_element_type=jnp.float32) + bias[case]
            col = lax.broadcasted_iota(jnp.int32, (TILE, TILE), 1)
            row = lax.broadcasted_iota(jnp.int32, (TILE, TILE), 0)
            s_old = jnp.where(col > row, scores[:, :TILE], LOW)
            s_mid = scores[:, TILE:WINDOW]
            s_new = jnp.where(col <= row, scores[:, WINDOW:], LOW)
            if not whole:
                place = lax.broadcasted_iota(jnp.int32, (TILE, WINDOW), 1)
                s_old = jnp.where(place[:, :TILE] >= outside, s_old, LOW)
                s_mid = jnp.where(place[:, TILE:] >= outside, s_mid, LOW)
            parts = [s_old, s_mid, s_new, s_far]
            tops = [jnp.max(part, axis=1, keepdims=True) for part in parts]
            top = jnp.maximum(jnp.maximum(tops[0], tops[1]), jnp.maximum(tops[2], tops[3]))
            weights = [jnp.exp2((part - top) * EXP_SCALE) for part in parts]
            total = sum(jnp.sum(part, axis=1, keepdims=True) for part in weights)
            rounded = [part.astype(jnp.bfloat16) for part in weights]
            mixed = jnp.dot(
                jnp.concatenate(rounded[:3], axis=1), kv[1, near, :], preferred_element_type=jnp.float32
            )
            mixed = mixed + jnp.dot(rounded[3], far[1], preferred_element_type=jnp.float32)
            o_all[here, :] = (mixed / total).astype(jnp.bfloat16)

        @pl.when(outside > 0)
        def _():
            attend(False)

        @pl.when(outside <= 0)
        def _():
            attend(True)

        target = out.at[:, cols(h * RING + x)]
        for e in range(2):
            r = 2 * half + lax.rem(h + e, 2)
            result = o_all.at[rows(j * BLK + r * PIECE, PIECE)]

            def send(result=result, r=r):
                pltpu.make_async_remote_copy(
                    src_ref=result,
                    dst_ref=target,
                    send_sem=o_send,
                    recv_sem=o_sem,
                    device_id=(first + j, r),
                    device_id_type=MESH,
                ).start()

            if e:
                send()
            else:
                mine = (dx == 0) & (d == 0)

                @pl.when(mine)
                def _():
                    pltpu.make_async_copy(result, target, o_sem).start()

                pl.when(jnp.logical_not(mine))(send)

        return carry

    lax.fori_loop(0, STEPS, step, 0)

    wait(kv.at[:, pl.ds(0, 3 * BLK)], send_sem.at[0])
    wait(q_all.at[pl.ds(0, 3 * BLK)], send_sem.at[1])
    pl.when(has_next)(functools.partial(wait, kv.at[:, pl.ds(0, WINDOW)], halo_send))
    for d in range(1, GROUPS):
        pl.when(group + d < GROUPS)(functools.partial(wait, far.at[:, pl.ds(d * SUMM, SUMM)], far_send.at[d]))
    wait(o_all.at[pl.ds(0, ROWS - PIECE)], o_send)
    wait(out, o_sem)


def on_device(queries, key_rows, value_rows):
    dma = pltpu.SemaphoreType.DMA
    return pl.pallas_call(
        kernel,
        name="attention",
        out_shape=jax.ShapeDtypeStruct((BLK // HEAD_DEV, HEAD_DEV * RING * HD), jnp.bfloat16),
        in_specs=[pl.BlockSpec(memory_space=pltpu.MemorySpace.HBM)] * 3,
        out_specs=pl.BlockSpec(memory_space=pltpu.MemorySpace.HBM),
        scratch_shapes=[
            pltpu.VMEM((ROWS, HD), jnp.bfloat16),
            pltpu.VMEM((2, WINDOW + ROWS, HD), jnp.bfloat16),
            pltpu.VMEM((2, FAR, HD), jnp.bfloat16),
            pltpu.VMEM((ROWS, HD), jnp.bfloat16),
            pltpu.VMEM((3, TILE, FAR), jnp.float32),
            dma((RING, PIECES)),
            dma((RING, HALF)),
            dma,
            dma((GROUPS,)),
            dma,
            dma((2,)),
            dma,
            dma((GROUPS,)),
            dma,
            pltpu.SemaphoreType.REGULAR,
            pltpu.SemaphoreType.REGULAR,
        ],
        compiler_params=pltpu.CompilerParams(
            collective_id=1, has_side_effects=True, vmem_limit_bytes=60 << 20
        ),
    )(queries, key_rows, value_rows)


def solution(mesh):
    placed = (P("ctx", "head"), P("ctx", "head"), P("ctx", "head"))
    return jax.shard_map(
        on_device, mesh=mesh, in_specs=placed, out_specs=P(("ctx", "head"), None), check_vma=False
    )
```

```python
import functools

import jax
import jax.numpy as jnp
from jax import lax
from jax.experimental import pallas as pl
from jax.experimental.pallas import tpu as pltpu
from jax.sharding import PartitionSpec as P

HD = 128
BLK = 512
RING = 4
HEAD_DEV = 4
ROWS = RING * BLK
WINDOW = 1024
SUMM = 16
GROUPS = 16
FAR_STEP = 1
VMEM_KIB = 54400
FAR = GROUPS * SUMM
TILE = 256
BAND = WINDOW + TILE
STEPS = ROWS // TILE
HALF = BLK // TILE
PIECES = 4
PIECE = BLK // PIECES
PEERS = (1, 3, 2)
ORDER = (3, 2, 1, 0)
LOW = -1e30
EXP_SCALE = HD**-0.5 * 1.4426950408889634
MESH = pl.DeviceIdType.MESH


def kernel(
    q_in, k_in, v_in, out, q_all, kv, far, o_all, bias,
    kv_sem, q_sem, halo_sem, far_sem, o_sem, send_sem, halo_send, far_send, o_send,
    halo_ready, far_ready,
):
    ctx, h = lax.axis_index("ctx"), lax.axis_index("head")
    x, group = lax.rem(ctx, RING), ctx // RING
    first = ctx - x

    def ring(dx):
        return lax.rem(x + dx + RING, RING)

    layers = GROUPS // 2
    depth = lax.rem(group, layers)
    rank = 2 * depth + group // layers

    def ranked(place):
        return ((lax.rem(place, 2) * layers + place // 2) * RING + x, h)

    def group_peer(d):
        return (lax.rem(ctx + RING * d, RING * GROUPS), h)

    def cols(place):
        return pl.ds(pl.multiple_of(place * HD, HD), HD)

    def rows(start, size):
        return pl.ds(pl.multiple_of(start, PIECE), size)

    def wait(ref, sem):
        pltpu.make_async_copy(ref, ref, sem).wait()

    def half_of(d):
        return lax.rem(h // 2 + d, HALF)

    sources = ((0, k_in), (1, v_in))
    own = pl.ds(pl.multiple_of(WINDOW + x * BLK, BLK), BLK)
    for i, src in sources:
        pltpu.make_async_copy(src.at[:, cols(x)], kv.at[i, own], kv_sem.at[x, 0]).start()
    pltpu.make_async_copy(
        q_in.at[:, cols(x)], q_all.at[pl.ds(pl.multiple_of(x * BLK, BLK), BLK)], q_sem.at[0, 0]
    ).start()

    far[...] = jnp.zeros_like(far)

    @pl.when(group == 0)
    def _():
        kv[:, 0:WINDOW, :] = jnp.zeros((2, WINDOW, HD), jnp.bfloat16)

    barrier = pltpu.get_barrier_semaphore()
    partners = 0
    for dx in range(RING):
        for dh in range(HEAD_DEV):
            if dx or dh:
                pl.semaphore_signal(
                    barrier, inc=1, device_id=(first + ring(dx), lax.rem(h + dh, HEAD_DEV)),
                    device_id_type=MESH,
                )
                partners += 1
    for e in range(1, GROUPS):
        @pl.when(rank + e < GROUPS)
        def _():
            pl.semaphore_signal(barrier, inc=1, device_id=ranked(rank + e), device_id_type=MESH)

    col = lax.broadcasted_iota(jnp.int32, (TILE, FAR), 1)
    row = lax.broadcasted_iota(jnp.int32, (TILE, FAR), 0)
    known = (col >= SUMM) & (col < SUMM * (group + 1))
    for case in range(3):
        seen = known
        if case == 0:
            seen = known & (col >= 2 * SUMM)
        if case == 1:
            seen = known & ((col >= 2 * SUMM) | (col - SUMM <= row - (TILE - SUMM)))
        bias[case] = jnp.where(seen, 0.0, LOW)

    pl.semaphore_wait(barrier, partners + rank)
    for e in range(1, GROUPS):
        place = jnp.maximum(rank - e, 0)
        source = lax.rem(place, 2) * layers + place // 2

        @pl.when((e <= rank) & (source < group - 1))
        def _():
            pl.semaphore_signal(far_ready, inc=1, device_id=ranked(place), device_id_type=MESH)

        @pl.when((e <= rank) & (source == group - 1))
        def _():
            pl.semaphore_signal(halo_ready, inc=1, device_id=ranked(place), device_id_type=MESH)


    def send_kv(p):
        for dx in PEERS:
            place = ring(dx)
            for i, src in sources:
                pltpu.make_async_remote_copy(
                    src_ref=src.at[pl.ds(p * PIECE, PIECE), cols(place)],
                    dst_ref=kv.at[i, rows(WINDOW + x * BLK + p * PIECE, PIECE)],
                    send_sem=send_sem.at[0],
                    recv_sem=kv_sem.at[x, p],
                    device_id=(first + place, h),
                    device_id_type=MESH,
                ).start()

    def send_q(d):
        half = half_of(d)
        for dx in PEERS:
            place = ring(dx)
            pltpu.make_async_remote_copy(
                src_ref=q_in.at[rows(half * TILE, TILE), cols(place)],
                dst_ref=q_all.at[rows(x * BLK + half * TILE, TILE)],
                send_sem=send_sem.at[1],
                recv_sem=q_sem.at[dx, d],
                device_id=(first + place, h),
                device_id_type=MESH,
            ).start()

    rounds = [functools.partial(send_kv, p) for p in ORDER]
    ahead = 4
    for send in rounds[:ahead]:
        send()

    def to_next(j, start, size):
        return pltpu.make_async_remote_copy(
            src_ref=kv.at[:, rows(WINDOW + j * BLK + start, size)],
            dst_ref=kv.at[:, rows((j - 2) * BLK + start, size)],
            send_sem=halo_send,
            recv_sem=halo_sem,
            device_id=group_peer(1),
            device_id_type=MESH,
        )

    def summary(d):
        return pltpu.make_async_remote_copy(
            src_ref=kv.at[:, pl.ds(WINDOW + ROWS - SUMM, SUMM)],
            dst_ref=far.at[:, pl.ds(d * SUMM, SUMM)],
            send_sem=far_send.at[d],
            recv_sem=far_sem.at[d],
            device_id=group_peer(d),
            device_id_type=MESH,
        )

    def arrived(j, p):
        wait(kv.at[:, pl.ds(0, PIECE)], kv_sem.at[j, p])

    has_next = group < GROUPS - 1

    @pl.when(depth < layers - 1)
    def _():
        pl.semaphore_wait(halo_ready, 1)

    @pl.when(x >= 2)
    def _():
        wait(kv.at[:, pl.ds(0, BLK)], kv_sem.at[x, 0])

        @pl.when(has_next)
        def _():
            to_next(x, 0, BLK).start()

    for step, p in enumerate(ORDER):
        for j in (3, 2):
            @pl.when(x != j)
            def _():
                arrived(j, p)

            @pl.when(has_next & (x != j))
            def _():
                to_next(j, p * PIECE, PIECE).start()

        if step == 0:
            for d in range(1, GROUPS):
                pl.when((group + d < GROUPS) & (lax.rem(group + d, layers) < depth))(summary(d).start)
        if step == FAR_STEP:
            later = jnp.where(group < layers, GROUPS - 1 - 2 * depth, layers - 1 - depth)
            ready = later - jnp.where(depth < layers - 1, 1, 0)

            @pl.when(ready > 0)
            def _():
                pl.semaphore_wait(far_ready, ready)

            for d in range(1, GROUPS):
                pl.when((group + d < GROUPS) & (lax.rem(group + d, layers) >= depth))(summary(d).start)
        if ahead + step < len(rounds):
            rounds[ahead + step]()
    send_q(0)
    wait(q_all.at[pl.ds(0, BLK)], q_sem.at[0, 0])

    @pl.when(x < 2)
    def _():
        wait(kv.at[:, pl.ds(0, BLK)], kv_sem.at[x, 0])

    for p in ORDER:
        for j in (0, 1):
            @pl.when(x != j)
            def _():
                arrived(j, p)

    send_q(1)
    for d in range(1, GROUPS):
        pl.when(d <= group)(functools.partial(wait, far.at[:, pl.ds(d * SUMM, SUMM)], far_sem.at[d]))

    patient = group == layers

    def step(s, carry):
        u = jnp.maximum(s - 2, 0)
        i = lax.rem(u, 3)
        late_j = jnp.where(s < 2, x, jnp.where(i == 0, 5 - x, i - 1))
        late_d = jnp.where(s < 2, s, u // 3)
        i = jnp.maximum(s - 5, 0)
        early_j = jnp.where(
            s < 2, 2 + s, jnp.where(s < 4, x, jnp.where((s == 4) | (i == 2), 1 - x, 2 + i))
        )
        early_d = jnp.where((s < 2) | (s == 4), 0, jnp.where(s < 4, s - 2, 1))
        u = jnp.maximum(s - 4, 0)
        last_j = jnp.where(
            x >= 2, jnp.where(s < 2, x, jnp.where(s < 4, 5 - x, lax.rem(u, 2))),
            jnp.where(s < 4, 2 + lax.rem(s, 2), jnp.where(s < 6, x, 1 - x)),
        )
        last_d = jnp.where(
            x >= 2, jnp.where(s < 4, lax.rem(s, 2), u // 2),
            jnp.where(s < 4, s // 2, lax.rem(s, 2)),
        )
        j = jnp.where(patient, last_j, jnp.where(x >= 2, late_j, early_j))
        d = jnp.where(patient, last_d, jnp.where(x >= 2, late_d, early_d))
        dx = lax.rem(x - j + RING, RING)
        half = half_of(d)
        t = j * HALF + half
        here = rows(t * TILE, TILE)

        @pl.when((s == jnp.where(patient, 4, jnp.where(x >= 2, 3, 2))) & (group > 0))
        def _():
            wait(kv.at[:, pl.ds(0, WINDOW)], halo_sem)

        @pl.when(dx > 0)
        def _():
            wait(q_all.at[pl.ds(0, TILE)], q_sem.at[dx, d])

        case = jnp.where(t < 3, 0, jnp.where(t == 3, 1, 2))
        outside = jnp.where(group == 0, WINDOW - t * TILE, 0)

        def attend(whole):
            q = q_all[here, :]
            nt = (((1,), (1,)), ((), ()))
            near = rows(t * TILE, BAND)
            scores = lax.dot_general(q, kv[0, near, :], nt, preferred_element_type=jnp.float32)
            s_far = lax.dot_general(q, far[0], nt, preferred_element_type=jnp.float32) + bias[case]
            col = lax.broadcasted_iota(jnp.int32, (TILE, TILE), 1)
            row = lax.broadcasted_iota(jnp.int32, (TILE, TILE), 0)
            s_old = jnp.where(col > row, scores[:, :TILE], LOW)
            s_mid = scores[:, TILE:WINDOW]
            s_new = jnp.where(col <= row, scores[:, WINDOW:], LOW)
            if not whole:
                place = lax.broadcasted_iota(jnp.int32, (TILE, WINDOW), 1)
                s_old = jnp.where(place[:, :TILE] >= outside, s_old, LOW)
                s_mid = jnp.where(place[:, TILE:] >= outside, s_mid, LOW)
            parts = [s_old, s_mid, s_new, s_far]
            tops = [jnp.max(part, axis=1, keepdims=True) for part in parts]
            top = jnp.maximum(jnp.maximum(tops[0], tops[1]), jnp.maximum(tops[2], tops[3]))
            weights = [jnp.exp2((part - top) * EXP_SCALE) for part in parts]
            total = sum(jnp.sum(part, axis=1, keepdims=True) for part in weights)
            rounded = [part.astype(jnp.bfloat16) for part in weights]
            mixed = jnp.dot(
                jnp.concatenate(rounded[:3], axis=1), kv[1, near, :], preferred_element_type=jnp.float32
            )
            mixed = mixed + jnp.dot(rounded[3], far[1], preferred_element_type=jnp.float32)
            o_all[here, :] = (mixed / total).astype(jnp.bfloat16)

        @pl.when(outside > 0)
        def _():
            attend(False)

        @pl.when(outside <= 0)
        def _():
            attend(True)

        target = out.at[:, cols(h * RING + x)]
        for e in range(2):
            r = 2 * half + lax.rem(h + e, 2)
            result = o_all.at[rows(j * BLK + r * PIECE, PIECE)]

            def send(result=result, r=r):
                pltpu.make_async_remote_copy(
                    src_ref=result,
                    dst_ref=target,
                    send_sem=o_send,
                    recv_sem=o_sem,
                    device_id=(first + j, r),
                    device_id_type=MESH,
                ).start()

            if e:
                send()
            else:
                mine = (dx == 0) & (d == 0)

                @pl.when(mine)
                def _():
                    pltpu.make_async_copy(result, target, o_sem).start()

                pl.when(jnp.logical_not(mine))(send)

        return carry

    lax.fori_loop(0, STEPS, step, 0)

    wait(kv.at[:, pl.ds(0, 3 * BLK)], send_sem.at[0])
    wait(q_all.at[pl.ds(0, 3 * BLK)], send_sem.at[1])
    pl.when(has_next)(functools.partial(wait, kv.at[:, pl.ds(0, WINDOW)], halo_send))
    for d in range(1, GROUPS):
        pl.when(group + d < GROUPS)(functools.partial(wait, far.at[:, pl.ds(d * SUMM, SUMM)], far_send.at[d]))
    wait(o_all.at[pl.ds(0, ROWS - PIECE)], o_send)
    wait(out, o_sem)


def on_device(queries, key_rows, value_rows):
    dma = pltpu.SemaphoreType.DMA
    return pl.pallas_call(
        kernel,
        name="attention",
        out_shape=jax.ShapeDtypeStruct((BLK // HEAD_DEV, HEAD_DEV * RING * HD), jnp.bfloat16),
        in_specs=[pl.BlockSpec(memory_space=pltpu.MemorySpace.HBM)] * 3,
        out_specs=pl.BlockSpec(memory_space=pltpu.VMEM),
        scratch_shapes=[
            pltpu.VMEM((ROWS, HD), jnp.bfloat16),
            pltpu.VMEM((2, WINDOW + ROWS, HD), jnp.bfloat16),
            pltpu.VMEM((2, FAR, HD), jnp.bfloat16),
            pltpu.VMEM((ROWS, HD), jnp.bfloat16),
            pltpu.VMEM((3, TILE, FAR), jnp.float32),
            dma((RING, PIECES)),
            dma((RING, HALF)),
            dma,
            dma((GROUPS,)),
            dma,
            dma((2,)),
            dma,
            dma((GROUPS,)),
            dma,
            pltpu.SemaphoreType.REGULAR,
            pltpu.SemaphoreType.REGULAR,
        ],
        compiler_params=pltpu.CompilerParams(
            collective_id=1, has_side_effects=True, vmem_limit_bytes=VMEM_KIB << 10
        ),
    )(queries, key_rows, value_rows)


def solution(mesh):
    placed = (P("ctx", "head"), P("ctx", "head"), P("ctx", "head"))
    return jax.shard_map(
        on_device, mesh=mesh, in_specs=placed, out_specs=P(("ctx", "head"), None), check_vma=False
    )
```

```python
import functools

import jax
import jax.numpy as jnp
from jax import lax
from jax.experimental import pallas as pl
from jax.experimental.pallas import tpu as pltpu
from jax.sharding import PartitionSpec as P

HD = 128
BLK = 512
RING = 4
HEAD_DEV = 4
ROWS = RING * BLK
WINDOW = 1024
SUMM = 16
GROUPS = 16
FAR_STEP = 2
VMEM_KIB = 54400
FAR = GROUPS * SUMM
TILE = 256
BAND = WINDOW + TILE
STEPS = ROWS // TILE
HALF = BLK // TILE
PIECES = 4
PIECE = BLK // PIECES
PEERS = (1, 3, 2)
PARTS = 8
PART = BLK // PARTS
ORDER = tuple(reversed(range(PARTS)))
LOW = -1e30
EXP_SCALE = HD**-0.5 * 1.4426950408889634
MESH = pl.DeviceIdType.MESH


def kernel(
    q_in, k_in, v_in, out, q_all, kv, far, o_all, bias,
    kv_sem, q_sem, halo_sem, far_sem, o_sem, send_sem, halo_send, far_send, o_send,
    halo_ready, far_ready,
):
    ctx, h = lax.axis_index("ctx"), lax.axis_index("head")
    x, group = lax.rem(ctx, RING), ctx // RING
    first = ctx - x

    def ring(dx):
        return lax.rem(x + dx + RING, RING)

    layers = GROUPS // 2
    depth = lax.rem(group, layers)
    rank = 2 * depth + group // layers
    flip = jnp.where(depth > 0, 1, 0)

    def ranked(place):
        return ((lax.rem(place, 2) * layers + place // 2) * RING + x, h)

    def group_peer(d):
        return (lax.rem(ctx + RING * d, RING * GROUPS), h)

    def cols(place):
        return pl.ds(pl.multiple_of(place * HD, HD), HD)

    def rows(start, size):
        return pl.ds(pl.multiple_of(start, PART), size)

    def wait(ref, sem):
        pltpu.make_async_copy(ref, ref, sem).wait()

    def half_of(d):
        return lax.rem(h // 2 + flip + d, HALF)

    sources = ((0, k_in), (1, v_in))
    own = pl.ds(pl.multiple_of(WINDOW + x * BLK, BLK), BLK)
    for i, src in sources:
        pltpu.make_async_copy(src.at[:, cols(x)], kv.at[i, own], kv_sem.at[x, 0]).start()
    pltpu.make_async_copy(
        q_in.at[:, cols(x)], q_all.at[pl.ds(pl.multiple_of(x * BLK, BLK), BLK)], q_sem.at[0, 0]
    ).start()

    far[...] = jnp.zeros_like(far)

    @pl.when(group == 0)
    def _():
        kv[:, 0:WINDOW, :] = jnp.zeros((2, WINDOW, HD), jnp.bfloat16)

    barrier = pltpu.get_barrier_semaphore()
    partners = 0
    for dx in range(RING):
        for dh in range(HEAD_DEV):
            if dx or dh:
                pl.semaphore_signal(
                    barrier, inc=1, device_id=(first + ring(dx), lax.rem(h + dh, HEAD_DEV)),
                    device_id_type=MESH,
                )
                partners += 1
    for e in range(1, GROUPS):
        @pl.when(rank + e < GROUPS)
        def _():
            pl.semaphore_signal(barrier, inc=1, device_id=ranked(rank + e), device_id_type=MESH)

    col = lax.broadcasted_iota(jnp.int32, (TILE, FAR), 1)
    row = lax.broadcasted_iota(jnp.int32, (TILE, FAR), 0)
    known = (col >= SUMM) & (col < SUMM * (group + 1))
    for case in range(3):
        seen = known
        if case == 0:
            seen = known & (col >= 2 * SUMM)
        if case == 1:
            seen = known & ((col >= 2 * SUMM) | (col - SUMM <= row - (TILE - SUMM)))
        bias[case] = jnp.where(seen, 0.0, LOW)

    pl.semaphore_wait(barrier, partners + rank)

    def send_kv(p):
        for dx in PEERS:
            place = ring(dx)
            for i, src in sources:
                pltpu.make_async_remote_copy(
                    src_ref=src.at[pl.ds(p * PART, PART), cols(place)],
                    dst_ref=kv.at[i, rows(WINDOW + x * BLK + p * PART, PART)],
                    send_sem=send_sem.at[0],
                    recv_sem=kv_sem.at[x, p],
                    device_id=(first + place, h),
                    device_id_type=MESH,
                ).start()

    def send_q(d):
        half = half_of(d)
        for dx in PEERS:
            place = ring(dx)
            pltpu.make_async_remote_copy(
                src_ref=q_in.at[rows(half * TILE, TILE), cols(place)],
                dst_ref=q_all.at[rows(x * BLK + half * TILE, TILE)],
                send_sem=send_sem.at[1],
                recv_sem=q_sem.at[dx, d],
                device_id=(first + place, h),
                device_id_type=MESH,
            ).start()

    rounds = [functools.partial(send_kv, p) for p in ORDER]
    ahead = 4
    for send in rounds[:ahead]:
        send()

    for e in range(1, GROUPS):
        place = jnp.maximum(rank - e, 0)
        source = lax.rem(place, 2) * layers + place // 2

        @pl.when((e <= rank) & (source < group - 1))
        def _():
            pl.semaphore_signal(far_ready, inc=1, device_id=ranked(place), device_id_type=MESH)

        @pl.when((e <= rank) & (source == group - 1))
        def _():
            pl.semaphore_signal(halo_ready, inc=1, device_id=ranked(place), device_id_type=MESH)

    def to_next(j, start, size):
        return pltpu.make_async_remote_copy(
            src_ref=kv.at[:, rows(WINDOW + j * BLK + start, size)],
            dst_ref=kv.at[:, rows((j - 2) * BLK + start, size)],
            send_sem=halo_send,
            recv_sem=halo_sem,
            device_id=group_peer(1),
            device_id_type=MESH,
        )

    def summary(d):
        return pltpu.make_async_remote_copy(
            src_ref=kv.at[:, pl.ds(WINDOW + ROWS - SUMM, SUMM)],
            dst_ref=far.at[:, pl.ds(d * SUMM, SUMM)],
            send_sem=far_send.at[d],
            recv_sem=far_sem.at[d],
            device_id=group_peer(d),
            device_id_type=MESH,
        )

    def arrived(j, p):
        wait(kv.at[:, pl.ds(0, PART)], kv_sem.at[j, p])

    has_next = group < GROUPS - 1

    @pl.when(depth < layers - 1)
    def _():
        pl.semaphore_wait(halo_ready, 1)

    @pl.when(x >= 2)
    def _():
        wait(kv.at[:, pl.ds(0, BLK)], kv_sem.at[x, 0])

        @pl.when(has_next)
        def _():
            to_next(x, 0, BLK).start()

    for step, p in enumerate(ORDER):
        for j in (3, 2):
            @pl.when(x != j)
            def _():
                arrived(j, p)

            @pl.when(has_next & (x != j))
            def _():
                to_next(j, p * PART, PART).start()

        if step == 0:
            for d in range(1, GROUPS):
                pl.when((group + d < GROUPS) & (lax.rem(group + d, layers) < depth))(summary(d).start)
        if step == FAR_STEP:
            later = jnp.where(group < layers, GROUPS - 1 - 2 * depth, layers - 1 - depth)
            ready = later - jnp.where(depth < layers - 1, 1, 0)

            @pl.when(ready > 0)
            def _():
                pl.semaphore_wait(far_ready, ready)

            for d in range(1, GROUPS):
                pl.when((group + d < GROUPS) & (lax.rem(group + d, layers) >= depth))(summary(d).start)
        if ahead + step < len(rounds):
            rounds[ahead + step]()
    send_q(0)
    wait(q_all.at[pl.ds(0, BLK)], q_sem.at[0, 0])

    @pl.when(x < 2)
    def _():
        wait(kv.at[:, pl.ds(0, BLK)], kv_sem.at[x, 0])

    for p in ORDER:
        for j in (0, 1):
            @pl.when(x != j)
            def _():
                arrived(j, p)

    send_q(1)
    for d in range(1, GROUPS):
        pl.when(d <= group)(functools.partial(wait, far.at[:, pl.ds(d * SUMM, SUMM)], far_sem.at[d]))

    patient = group == layers
    odd = lax.rem(x, 2)

    def step(s, carry):
        u = jnp.maximum(s - 2, 0)
        i = lax.rem(u, 3)
        late_j = jnp.where(s < 2, x, jnp.where(i == 0, 5 - x, lax.rem(i + 1 + odd, 2)))
        late_d = jnp.where(s < 2, s, u // 3)
        i = jnp.maximum(s - 5, 0)
        early_j = jnp.where(
            s < 2, 2 + lax.rem(s + odd, 2),
            jnp.where(s < 4, x, jnp.where((s == 4) | (i == 2), 1 - x, 2 + lax.rem(i + odd, 2))),
        )
        early_d = jnp.where((s < 2) | (s == 4), 0, jnp.where(s < 4, s - 2, 1))
        u = jnp.maximum(s - 4, 0)
        last_j = jnp.where(
            x >= 2, jnp.where(s < 2, x, jnp.where(s < 4, 5 - x, lax.rem(u + odd, 2))),
            jnp.where(s < 4, 2 + lax.rem(s + odd, 2), jnp.where(s < 6, x, 1 - x)),
        )
        last_d = jnp.where(
            x >= 2, jnp.where(s < 4, lax.rem(s, 2), u // 2),
            jnp.where(s < 4, s // 2, lax.rem(s, 2)),
        )
        j = jnp.where(patient, last_j, jnp.where(x >= 2, late_j, early_j))
        d = jnp.where(patient, last_d, jnp.where(x >= 2, late_d, early_d))
        dx = lax.rem(x - j + RING, RING)
        half = half_of(d)
        t = j * HALF + half
        here = rows(t * TILE, TILE)

        @pl.when((s == jnp.where(patient, 4, jnp.where(x >= 2, 3, 2))) & (group > 0))
        def _():
            wait(kv.at[:, pl.ds(0, WINDOW)], halo_sem)

        @pl.when(dx > 0)
        def _():
            wait(q_all.at[pl.ds(0, TILE)], q_sem.at[dx, d])

        case = jnp.where(t < 3, 0, jnp.where(t == 3, 1, 2))
        outside = jnp.where(group == 0, WINDOW - t * TILE, 0)

        def attend(whole):
            q = q_all[here, :]
            nt = (((1,), (1,)), ((), ()))
            skip = 0 if whole else TILE
            near = rows(t * TILE + skip, BAND - skip)
            scores = lax.dot_general(q, kv[0, near, :], nt, preferred_element_type=jnp.float32)
            s_far = lax.dot_general(q, far[0], nt, preferred_element_type=jnp.float32) + bias[case]
            col = lax.broadcasted_iota(jnp.int32, (TILE, TILE), 1)
            row = lax.broadcasted_iota(jnp.int32, (TILE, TILE), 0)
            s_mid = scores[:, TILE - skip : WINDOW - skip]
            s_new = jnp.where(col <= row, scores[:, WINDOW - skip :], LOW)
            if whole:
                s_old = jnp.where(col > row, scores[:, :TILE], LOW)
                parts = [s_old, s_mid, s_new, s_far]
            else:
                place = lax.broadcasted_iota(jnp.int32, (1, WINDOW - TILE), 1) + TILE
                parts = [s_mid + jnp.where(place >= outside, 0.0, LOW), s_new, s_far]
            top = functools.reduce(jnp.maximum, [jnp.max(part, axis=1, keepdims=True) for part in parts])
            weights = [jnp.exp2((part - top) * EXP_SCALE) for part in parts]
            total = sum(jnp.sum(part, axis=1, keepdims=True) for part in weights)
            rounded = [part.astype(jnp.bfloat16) for part in weights]
            mixed = jnp.dot(
                jnp.concatenate(rounded[:-1], axis=1), kv[1, near, :], preferred_element_type=jnp.float32
            )
            mixed = mixed + jnp.dot(rounded[-1], far[1], preferred_element_type=jnp.float32)
            o_all[here, :] = (mixed / total).astype(jnp.bfloat16)

        @pl.when(outside > 0)
        def _():
            attend(False)

        @pl.when(outside <= 0)
        def _():
            attend(True)

        target = out.at[:, cols(h * RING + x)]
        for e in range(2):
            r = 2 * half + lax.rem(h + e, 2)
            result = o_all.at[rows(j * BLK + r * PIECE, PIECE)]

            def send(result=result, r=r):
                pltpu.make_async_remote_copy(
                    src_ref=result,
                    dst_ref=target,
                    send_sem=o_send,
                    recv_sem=o_sem,
                    device_id=(first + j, r),
                    device_id_type=MESH,
                ).start()

            if e:
                send()
            else:
                mine = (dx == 0) & (d == flip)

                @pl.when(mine)
                def _():
                    pltpu.make_async_copy(result, target, o_sem).start()

                pl.when(jnp.logical_not(mine))(send)

        return carry

    lax.fori_loop(0, STEPS, step, 0)

    wait(kv.at[:, pl.ds(0, 3 * BLK)], send_sem.at[0])
    wait(q_all.at[pl.ds(0, 3 * BLK)], send_sem.at[1])
    pl.when(has_next)(functools.partial(wait, kv.at[:, pl.ds(0, WINDOW)], halo_send))
    for d in range(1, GROUPS):
        pl.when(group + d < GROUPS)(functools.partial(wait, far.at[:, pl.ds(d * SUMM, SUMM)], far_send.at[d]))
    wait(o_all.at[pl.ds(0, ROWS - PIECE)], o_send)
    wait(out, o_sem)


def on_device(queries, key_rows, value_rows):
    dma = pltpu.SemaphoreType.DMA
    return pl.pallas_call(
        kernel,
        name="attention",
        out_shape=jax.ShapeDtypeStruct((BLK // HEAD_DEV, HEAD_DEV * RING * HD), jnp.bfloat16),
        in_specs=[pl.BlockSpec(memory_space=pltpu.MemorySpace.HBM)] * 3,
        out_specs=pl.BlockSpec(memory_space=pltpu.VMEM),
        scratch_shapes=[
            pltpu.VMEM((ROWS, HD), jnp.bfloat16),
            pltpu.VMEM((2, WINDOW + ROWS, HD), jnp.bfloat16),
            pltpu.VMEM((2, FAR, HD), jnp.bfloat16),
            pltpu.VMEM((ROWS, HD), jnp.bfloat16),
            pltpu.VMEM((3, TILE, FAR), jnp.float32),
            dma((RING, PARTS)),
            dma((RING, HALF)),
            dma,
            dma((GROUPS,)),
            dma,
            dma((2,)),
            dma,
            dma((GROUPS,)),
            dma,
            pltpu.SemaphoreType.REGULAR,
            pltpu.SemaphoreType.REGULAR,
        ],
        compiler_params=pltpu.CompilerParams(
            collective_id=1, has_side_effects=True, vmem_limit_bytes=VMEM_KIB << 10
        ),
    )(queries, key_rows, value_rows)


def solution(mesh):
    placed = (P("ctx", "head"), P("ctx", "head"), P("ctx", "head"))
    return jax.shard_map(
        on_device, mesh=mesh, in_specs=placed, out_specs=P(("ctx", "head"), None), check_vma=False
    )
```

```python
import functools

import jax
import jax.numpy as jnp
from jax import lax
from jax.experimental import pallas as pl
from jax.experimental.pallas import tpu as pltpu
from jax.sharding import PartitionSpec as P

HD = 128
BLK = 512
RING = 4
HEAD_DEV = 4
ROWS = RING * BLK
WINDOW = 1024
SUMM = 16
GROUPS = 16
FAR_STEP = 2
VMEM_KIB = 54400
FAR = GROUPS * SUMM
TILE = 256
BAND = WINDOW + TILE
STEPS = ROWS // TILE
HALF = BLK // TILE
PIECES = 4
PIECE = BLK // PIECES
PEERS = (1, 3, 2)
PARTS = 8
PART = BLK // PARTS
ORDER = tuple(reversed(range(PARTS)))
LOW = -1e30
EXP_SCALE = HD**-0.5 * 1.4426950408889634
MESH = pl.DeviceIdType.MESH


def kernel(
    q_in, k_in, v_in, out, q_all, kv, far, o_all, bias,
    kv_sem, q_sem, halo_sem, far_sem, o_sem, send_sem, halo_send, far_send, o_send,
    halo_ready, far_ready,
):
    ctx, h = lax.axis_index("ctx"), lax.axis_index("head")
    x, group = lax.rem(ctx, RING), ctx // RING
    first = ctx - x

    def ring(dx):
        return lax.rem(x + dx + RING, RING)

    layers = GROUPS // 2
    depth = lax.rem(group, layers)
    rank = 2 * depth + group // layers
    flip = jnp.where(depth > 0, 1, 0)

    def ranked(place):
        return ((lax.rem(place, 2) * layers + place // 2) * RING + x, h)

    def group_peer(d):
        return (lax.rem(ctx + RING * d, RING * GROUPS), h)

    def cols(place):
        return pl.ds(pl.multiple_of(place * HD, HD), HD)

    def rows(start, size):
        return pl.ds(pl.multiple_of(start, PART), size)

    def wait(ref, sem):
        pltpu.make_async_copy(ref, ref, sem).wait()

    def half_of(d):
        return lax.rem(h // 2 + flip + d, HALF)

    sources = ((0, k_in), (1, v_in))
    own = pl.ds(pl.multiple_of(WINDOW + x * BLK, BLK), BLK)
    for i, src in sources:
        pltpu.make_async_copy(src.at[:, cols(x)], kv.at[i, own], kv_sem.at[x, 0]).start()
    pltpu.make_async_copy(
        q_in.at[:, cols(x)], q_all.at[pl.ds(pl.multiple_of(x * BLK, BLK), BLK)], q_sem.at[0, 0]
    ).start()

    far[...] = jnp.zeros_like(far)

    @pl.when(group == 0)
    def _():
        kv[:, 0:WINDOW, :] = jnp.zeros((2, WINDOW, HD), jnp.bfloat16)

    barrier = pltpu.get_barrier_semaphore()
    partners = 0
    for dx in range(RING):
        for dh in range(HEAD_DEV):
            if dx or dh:
                pl.semaphore_signal(
                    barrier, inc=1, device_id=(first + ring(dx), lax.rem(h + dh, HEAD_DEV)),
                    device_id_type=MESH,
                )
                partners += 1
    for e in range(1, GROUPS):
        @pl.when(rank + e < GROUPS)
        def _():
            pl.semaphore_signal(barrier, inc=1, device_id=ranked(rank + e), device_id_type=MESH)

    col = lax.broadcasted_iota(jnp.int32, (TILE, FAR), 1)
    row = lax.broadcasted_iota(jnp.int32, (TILE, FAR), 0)
    known = (col >= SUMM) & (col < SUMM * (group + 1))
    for case in range(3):
        seen = known
        if case == 0:
            seen = known & (col >= 2 * SUMM)
        if case == 1:
            seen = known & ((col >= 2 * SUMM) | (col - SUMM <= row - (TILE - SUMM)))
        bias[case] = jnp.where(seen, 0.0, LOW)

    pl.semaphore_wait(barrier, partners + rank)

    def send_kv(p):
        for dx in PEERS:
            place = ring(dx)
            for i, src in sources:
                pltpu.make_async_remote_copy(
                    src_ref=src.at[pl.ds(p * PART, PART), cols(place)],
                    dst_ref=kv.at[i, rows(WINDOW + x * BLK + p * PART, PART)],
                    send_sem=send_sem.at[0],
                    recv_sem=kv_sem.at[x, p],
                    device_id=(first + place, h),
                    device_id_type=MESH,
                ).start()

    def send_q(d):
        half = half_of(d)
        for dx in PEERS:
            place = ring(dx)
            pltpu.make_async_remote_copy(
                src_ref=q_in.at[rows(half * TILE, TILE), cols(place)],
                dst_ref=q_all.at[rows(x * BLK + half * TILE, TILE)],
                send_sem=send_sem.at[1],
                recv_sem=q_sem.at[dx, d],
                device_id=(first + place, h),
                device_id_type=MESH,
            ).start()

    rounds = [functools.partial(send_kv, p) for p in ORDER]
    ahead = 4
    for send in rounds[:ahead]:
        send()

    for e in range(1, GROUPS):
        place = jnp.maximum(rank - e, 0)
        source = lax.rem(place, 2) * layers + place // 2

        @pl.when((e <= rank) & (source < group - 1))
        def _():
            pl.semaphore_signal(far_ready, inc=1, device_id=ranked(place), device_id_type=MESH)

        @pl.when((e <= rank) & (source == group - 1))
        def _():
            pl.semaphore_signal(halo_ready, inc=1, device_id=ranked(place), device_id_type=MESH)

    def to_next(j, start, size):
        return pltpu.make_async_remote_copy(
            src_ref=kv.at[:, rows(WINDOW + j * BLK + start, size)],
            dst_ref=kv.at[:, rows((j - 2) * BLK + start, size)],
            send_sem=halo_send,
            recv_sem=halo_sem,
            device_id=group_peer(1),
            device_id_type=MESH,
        )

    def summary(d):
        return pltpu.make_async_remote_copy(
            src_ref=kv.at[:, pl.ds(WINDOW + ROWS - SUMM, SUMM)],
            dst_ref=far.at[:, pl.ds(d * SUMM, SUMM)],
            send_sem=far_send.at[d],
            recv_sem=far_sem.at[d],
            device_id=group_peer(d),
            device_id_type=MESH,
        )

    def arrived(j, p):
        wait(kv.at[:, pl.ds(0, PART)], kv_sem.at[j, p])

    has_next = group < GROUPS - 1

    @pl.when(depth < layers - 1)
    def _():
        pl.semaphore_wait(halo_ready, 1)

    @pl.when(x >= 2)
    def _():
        wait(kv.at[:, pl.ds(0, BLK)], kv_sem.at[x, 0])

        @pl.when(has_next)
        def _():
            to_next(x, 0, BLK).start()

    for step, p in enumerate(ORDER):
        for j in (3, 2):
            @pl.when(x != j)
            def _():
                arrived(j, p)

            @pl.when(has_next & (x != j))
            def _():
                to_next(j, p * PART, PART).start()

        if step == 0:
            for d in range(1, GROUPS):
                pl.when((group + d < GROUPS) & (lax.rem(group + d, layers) < depth))(summary(d).start)
        if step == FAR_STEP:
            later = jnp.where(group < layers, GROUPS - 1 - 2 * depth, layers - 1 - depth)
            ready = later - jnp.where(depth < layers - 1, 1, 0)

            @pl.when(ready > 0)
            def _():
                pl.semaphore_wait(far_ready, ready)

            for d in range(1, GROUPS):
                pl.when((group + d < GROUPS) & (lax.rem(group + d, layers) >= depth))(summary(d).start)
        if step == 5:
            pl.when(group != layers - 1)(functools.partial(send_q, 0))
        if ahead + step < len(rounds):
            rounds[ahead + step]()
    pl.when(group == layers - 1)(functools.partial(send_q, 0))
    wait(q_all.at[pl.ds(0, BLK)], q_sem.at[0, 0])

    @pl.when(x < 2)
    def _():
        wait(kv.at[:, pl.ds(0, BLK)], kv_sem.at[x, 0])

    for p in ORDER:
        for j in (0, 1):
            @pl.when(x != j)
            def _():
                arrived(j, p)

    send_q(1)
    for d in range(1, GROUPS):
        pl.when(d <= group)(functools.partial(wait, far.at[:, pl.ds(d * SUMM, SUMM)], far_sem.at[d]))

    patient = group == layers
    odd = lax.rem(x, 2)

    def step(s, carry):
        u = jnp.maximum(s - 2, 0)
        i = lax.rem(u, 3)
        late_j = jnp.where(s < 2, x, jnp.where(i == 0, 5 - x, lax.rem(i + 1 + odd, 2)))
        late_d = jnp.where(s < 2, s, u // 3)
        i = jnp.maximum(s - 5, 0)
        early_j = jnp.where(
            s < 2, 2 + lax.rem(s + odd, 2),
            jnp.where(s < 4, x, jnp.where((s == 4) | (i == 2), 1 - x, 2 + lax.rem(i + odd, 2))),
        )
        early_d = jnp.where((s < 2) | (s == 4), 0, jnp.where(s < 4, s - 2, 1))
        u = jnp.maximum(s - 4, 0)
        last_j = jnp.where(
            x >= 2, jnp.where(s < 2, x, jnp.where(s < 4, 5 - x, lax.rem(u + odd, 2))),
            jnp.where(s < 4, 2 + lax.rem(s + odd, 2), jnp.where(s < 6, x, 1 - x)),
        )
        last_d = jnp.where(
            x >= 2, jnp.where(s < 4, lax.rem(s, 2), 1 - u // 2),
            jnp.where(s < 4, s // 2, 1 - lax.rem(s, 2)),
        )
        j = jnp.where(patient, last_j, jnp.where(x >= 2, late_j, early_j))
        d = jnp.where(patient, last_d, jnp.where(x >= 2, late_d, early_d))
        dx = lax.rem(x - j + RING, RING)
        half = half_of(d)
        t = j * HALF + half
        here = rows(t * TILE, TILE)

        @pl.when((s == jnp.where(patient, 4, jnp.where(x >= 2, 3, 2))) & (group > 0))
        def _():
            wait(kv.at[:, pl.ds(0, WINDOW)], halo_sem)

        @pl.when(dx > 0)
        def _():
            wait(q_all.at[pl.ds(0, TILE)], q_sem.at[dx, d])

        case = jnp.where(t < 3, 0, jnp.where(t == 3, 1, 2))
        outside = jnp.where(group == 0, WINDOW - t * TILE, 0)

        def attend(whole):
            q = q_all[here, :]
            nt = (((1,), (1,)), ((), ()))
            skip = 0 if whole else TILE
            near = rows(t * TILE + skip, BAND - skip)
            scores = lax.dot_general(q, kv[0, near, :], nt, preferred_element_type=jnp.float32)
            s_far = lax.dot_general(q, far[0], nt, preferred_element_type=jnp.float32) + bias[case]
            col = lax.broadcasted_iota(jnp.int32, (TILE, TILE), 1)
            row = lax.broadcasted_iota(jnp.int32, (TILE, TILE), 0)
            s_mid = scores[:, TILE - skip : WINDOW - skip]
            s_new = jnp.where(col <= row, scores[:, WINDOW - skip :], LOW)
            if whole:
                s_old = jnp.where(col > row, scores[:, :TILE], LOW)
                parts = [s_old, s_mid, s_new, s_far]
            else:
                place = lax.broadcasted_iota(jnp.int32, (1, WINDOW - TILE), 1) + TILE
                parts = [s_mid + jnp.where(place >= outside, 0.0, LOW), s_new, s_far]
            top = functools.reduce(jnp.maximum, [jnp.max(part, axis=1, keepdims=True) for part in parts])
            weights = [jnp.exp2((part - top) * EXP_SCALE) for part in parts]
            total = sum(jnp.sum(part, axis=1, keepdims=True) for part in weights)
            rounded = [part.astype(jnp.bfloat16) for part in weights]
            mixed = jnp.dot(
                jnp.concatenate(rounded[:-1], axis=1), kv[1, near, :], preferred_element_type=jnp.float32
            )
            mixed = mixed + jnp.dot(rounded[-1], far[1], preferred_element_type=jnp.float32)
            o_all[here, :] = (mixed / total).astype(jnp.bfloat16)

        @pl.when(outside > 0)
        def _():
            attend(False)

        @pl.when(outside <= 0)
        def _():
            attend(True)

        target = out.at[:, cols(h * RING + x)]
        for e in range(2):
            r = 2 * half + lax.rem(h + e, 2)
            result = o_all.at[rows(j * BLK + r * PIECE, PIECE)]

            def send(result=result, r=r):
                pltpu.make_async_remote_copy(
                    src_ref=result,
                    dst_ref=target,
                    send_sem=o_send,
                    recv_sem=o_sem,
                    device_id=(first + j, r),
                    device_id_type=MESH,
                ).start()

            if e:
                send()
            else:
                mine = (dx == 0) & (d == flip)

                @pl.when(mine)
                def _():
                    pltpu.make_async_copy(result, target, o_sem).start()

                pl.when(jnp.logical_not(mine))(send)

        return carry

    lax.fori_loop(0, STEPS, step, 0)

    wait(kv.at[:, pl.ds(0, 3 * BLK)], send_sem.at[0])
    wait(q_all.at[pl.ds(0, 3 * BLK)], send_sem.at[1])
    pl.when(has_next)(functools.partial(wait, kv.at[:, pl.ds(0, WINDOW)], halo_send))
    for d in range(1, GROUPS):
        pl.when(group + d < GROUPS)(functools.partial(wait, far.at[:, pl.ds(d * SUMM, SUMM)], far_send.at[d]))
    wait(o_all.at[pl.ds(0, ROWS - PIECE)], o_send)
    wait(out, o_sem)


def on_device(queries, key_rows, value_rows):
    dma = pltpu.SemaphoreType.DMA
    return pl.pallas_call(
        kernel,
        name="attention",
        out_shape=jax.ShapeDtypeStruct((BLK // HEAD_DEV, HEAD_DEV * RING * HD), jnp.bfloat16),
        in_specs=[pl.BlockSpec(memory_space=pltpu.MemorySpace.HBM)] * 3,
        out_specs=pl.BlockSpec(memory_space=pltpu.VMEM),
        scratch_shapes=[
            pltpu.VMEM((ROWS, HD), jnp.bfloat16),
            pltpu.VMEM((2, WINDOW + ROWS, HD), jnp.bfloat16),
            pltpu.VMEM((2, FAR, HD), jnp.bfloat16),
            pltpu.VMEM((ROWS, HD), jnp.bfloat16),
            pltpu.VMEM((3, TILE, FAR), jnp.float32),
            dma((RING, PARTS)),
            dma((RING, HALF)),
            dma,
            dma((GROUPS,)),
            dma,
            dma((2,)),
            dma,
            dma((GROUPS,)),
            dma,
            pltpu.SemaphoreType.REGULAR,
            pltpu.SemaphoreType.REGULAR,
        ],
        compiler_params=pltpu.CompilerParams(
            collective_id=1, has_side_effects=True, vmem_limit_bytes=VMEM_KIB << 10
        ),
    )(queries, key_rows, value_rows)


def solution(mesh):
    placed = (P("ctx", "head"), P("ctx", "head"), P("ctx", "head"))
    return jax.shard_map(
        on_device, mesh=mesh, in_specs=placed, out_specs=P(("ctx", "head"), None), check_vma=False
    )
```

```python
import functools

import jax
import jax.numpy as jnp
from jax import lax
from jax.experimental import pallas as pl
from jax.experimental.pallas import tpu as pltpu
from jax.sharding import PartitionSpec as P

HD = 128
BLK = 512
RING = 4
HEAD_DEV = 4
ROWS = RING * BLK
WINDOW = 1024
SUMM = 16
GROUPS = 16
FAR_STEP = 2
VMEM_KIB = 54400
FAR = GROUPS * SUMM
TILE = 256
BAND = WINDOW + TILE
STEPS = ROWS // TILE
HALF = BLK // TILE
PIECES = 4
PIECE = BLK // PIECES
PEERS = (1, 3, 2)
PARTS = 8
PART = BLK // PARTS
ORDER = tuple(reversed(range(PARTS)))
LOW = -1e30
EXP_SCALE = HD**-0.5 * 1.4426950408889634
MESH = pl.DeviceIdType.MESH


def kernel(
    q_in, k_in, v_in, out, q_all, kv, far, o_all, bias,
    kv_sem, q_sem, halo_sem, far_sem, o_sem, send_sem, halo_send, far_send, o_send,
    halo_ready, far_ready,
):
    ctx, h = lax.axis_index("ctx"), lax.axis_index("head")
    x, group = lax.rem(ctx, RING), ctx // RING
    first = ctx - x

    def ring(dx):
        return lax.rem(x + dx + RING, RING)

    layers = GROUPS // 2
    depth = lax.rem(group, layers)
    rank = 2 * depth + group // layers
    flip = jnp.where(depth > 0, 1, 0)

    def ranked(place):
        return ((lax.rem(place, 2) * layers + place // 2) * RING + x, h)

    def group_peer(d):
        return (lax.rem(ctx + RING * d, RING * GROUPS), h)

    def cols(place):
        return pl.ds(pl.multiple_of(place * HD, HD), HD)

    def rows(start, size):
        return pl.ds(pl.multiple_of(start, PART), size)

    def wait(ref, sem):
        pltpu.make_async_copy(ref, ref, sem).wait()

    def half_of(d):
        return lax.rem(h // 2 + flip + d, HALF)

    sources = ((0, k_in), (1, v_in))
    own = pl.ds(pl.multiple_of(WINDOW + x * BLK, BLK), BLK)
    for i, src in sources:
        pltpu.make_async_copy(src.at[:, cols(x)], kv.at[i, own], kv_sem.at[x, 0]).start()
    pltpu.make_async_copy(
        q_in.at[:, cols(x)], q_all.at[pl.ds(pl.multiple_of(x * BLK, BLK), BLK)], q_sem.at[0, 0]
    ).start()

    far[...] = jnp.zeros_like(far)

    @pl.when(group == 0)
    def _():
        kv[:, 0:WINDOW, :] = jnp.zeros((2, WINDOW, HD), jnp.bfloat16)

    barrier = pltpu.get_barrier_semaphore()
    partners = 0
    for dx in range(RING):
        for dh in range(HEAD_DEV):
            if dx or dh:
                pl.semaphore_signal(
                    barrier, inc=1, device_id=(first + ring(dx), lax.rem(h + dh, HEAD_DEV)),
                    device_id_type=MESH,
                )
                partners += 1
    for e in range(1, GROUPS):
        @pl.when(rank + e < GROUPS)
        def _():
            pl.semaphore_signal(barrier, inc=1, device_id=ranked(rank + e), device_id_type=MESH)

    col = lax.broadcasted_iota(jnp.int32, (TILE, FAR), 1)
    row = lax.broadcasted_iota(jnp.int32, (TILE, FAR), 0)
    known = (col >= SUMM) & (col < SUMM * (group + 1))
    for case in range(3):
        seen = known
        if case == 0:
            seen = known & (col >= 2 * SUMM)
        if case == 1:
            seen = known & ((col >= 2 * SUMM) | (col - SUMM <= row - (TILE - SUMM)))
        bias[case] = jnp.where(seen, 0.0, LOW)

    pl.semaphore_wait(barrier, partners + rank)

    def send_kv(p):
        for dx in PEERS:
            place = ring(dx)
            for i, src in sources:
                pltpu.make_async_remote_copy(
                    src_ref=src.at[pl.ds(p * PART, PART), cols(place)],
                    dst_ref=kv.at[i, rows(WINDOW + x * BLK + p * PART, PART)],
                    send_sem=send_sem.at[0],
                    recv_sem=kv_sem.at[x, p],
                    device_id=(first + place, h),
                    device_id_type=MESH,
                ).start()

    def send_q(d):
        half = half_of(d)
        for dx in PEERS:
            place = ring(dx)
            pltpu.make_async_remote_copy(
                src_ref=q_in.at[rows(half * TILE, TILE), cols(place)],
                dst_ref=q_all.at[rows(x * BLK + half * TILE, TILE)],
                send_sem=send_sem.at[1],
                recv_sem=q_sem.at[dx, d],
                device_id=(first + place, h),
                device_id_type=MESH,
            ).start()

    rounds = [functools.partial(send_kv, p) for p in ORDER]
    ahead = 4
    for send in rounds[:ahead]:
        send()

    for e in range(1, GROUPS):
        place = jnp.maximum(rank - e, 0)
        source = lax.rem(place, 2) * layers + place // 2

        @pl.when((e <= rank) & (source < group - 1))
        def _():
            pl.semaphore_signal(far_ready, inc=1, device_id=ranked(place), device_id_type=MESH)

        @pl.when((e <= rank) & (source == group - 1))
        def _():
            pl.semaphore_signal(halo_ready, inc=1, device_id=ranked(place), device_id_type=MESH)

    def to_next(j, start, size):
        return pltpu.make_async_remote_copy(
            src_ref=kv.at[:, rows(WINDOW + j * BLK + start, size)],
            dst_ref=kv.at[:, rows((j - 2) * BLK + start, size)],
            send_sem=halo_send,
            recv_sem=halo_sem,
            device_id=group_peer(1),
            device_id_type=MESH,
        )

    def summary(d):
        return pltpu.make_async_remote_copy(
            src_ref=kv.at[:, pl.ds(WINDOW + ROWS - SUMM, SUMM)],
            dst_ref=far.at[:, pl.ds(d * SUMM, SUMM)],
            send_sem=far_send.at[d],
            recv_sem=far_sem.at[d],
            device_id=group_peer(d),
            device_id_type=MESH,
        )

    def arrived(j, p):
        wait(kv.at[:, pl.ds(0, PART)], kv_sem.at[j, p])

    has_next = group < GROUPS - 1

    @pl.when(depth < layers - 1)
    def _():
        pl.semaphore_wait(halo_ready, 1)

    @pl.when(x >= 2)
    def _():
        wait(kv.at[:, pl.ds(0, BLK)], kv_sem.at[x, 0])

        @pl.when(has_next)
        def _():
            to_next(x, 0, BLK).start()

    for step, p in enumerate(ORDER):
        for j in (3, 2):
            @pl.when(x != j)
            def _():
                arrived(j, p)

            @pl.when(has_next & (x != j))
            def _():
                to_next(j, p * PART, PART).start()

        if step == 0:
            for d in range(1, GROUPS):
                pl.when((group + d < GROUPS) & (lax.rem(group + d, layers) < depth))(summary(d).start)
        if step == FAR_STEP:
            later = jnp.where(group < layers, GROUPS - 1 - 2 * depth, layers - 1 - depth)
            ready = later - jnp.where(depth < layers - 1, 1, 0)

            @pl.when(ready > 0)
            def _():
                pl.semaphore_wait(far_ready, ready)

            for d in range(1, GROUPS):
                pl.when((group + d < GROUPS) & (lax.rem(group + d, layers) >= depth))(summary(d).start)
        if step == 3:
            pl.when(group != layers - 1)(functools.partial(send_q, 0))
        if ahead + step < len(rounds):
            rounds[ahead + step]()
    pl.when(group == layers - 1)(functools.partial(send_q, 0))
    wait(q_all.at[pl.ds(0, BLK)], q_sem.at[0, 0])

    @pl.when(x < 2)
    def _():
        wait(kv.at[:, pl.ds(0, BLK)], kv_sem.at[x, 0])

    for p in ORDER:
        for j in (0, 1):
            @pl.when(x != j)
            def _():
                arrived(j, p)

    send_q(1)
    for d in range(1, GROUPS):
        pl.when(d <= group)(functools.partial(wait, far.at[:, pl.ds(d * SUMM, SUMM)], far_sem.at[d]))

    patient = group == layers
    odd = lax.rem(x, 2)

    def step(s, carry):
        u = jnp.maximum(s - 2, 0)
        i = lax.rem(u, 3)
        late_j = jnp.where(s < 2, x, jnp.where(i == 0, 5 - x, lax.rem(i + 1 + odd, 2)))
        late_d = jnp.where(s < 2, s, u // 3)
        i = jnp.maximum(s - 5, 0)
        early_j = jnp.where(
            s < 2, 2 + lax.rem(s + odd, 2),
            jnp.where(s < 4, x, jnp.where((s == 4) | (i == 2), 1 - x, 2 + lax.rem(i + odd, 2))),
        )
        early_d = jnp.where((s < 2) | (s == 4), 0, jnp.where(s < 4, s - 2, 1))
        u = jnp.maximum(s - 4, 0)
        last_j = jnp.where(
            x >= 2, jnp.where(s < 2, x, jnp.where(s < 4, 5 - x, lax.rem(u + odd, 2))),
            jnp.where(s < 4, 2 + lax.rem(s + odd, 2), jnp.where(s < 6, x, 1 - x)),
        )
        last_d = jnp.where(
            x >= 2, jnp.where(s < 4, lax.rem(s, 2), 1 - u // 2),
            jnp.where(s < 4, s // 2, 1 - lax.rem(s, 2)),
        )
        j = jnp.where(patient, last_j, jnp.where(x >= 2, late_j, early_j))
        d = jnp.where(patient, last_d, jnp.where(x >= 2, late_d, early_d))
        dx = lax.rem(x - j + RING, RING)
        half = half_of(d)
        t = j * HALF + half
        here = rows(t * TILE, TILE)

        @pl.when((s == jnp.where(patient, 4, jnp.where(x >= 2, 3, 2))) & (group > 0))
        def _():
            wait(kv.at[:, pl.ds(0, WINDOW)], halo_sem)

        @pl.when(dx > 0)
        def _():
            wait(q_all.at[pl.ds(0, TILE)], q_sem.at[dx, d])

        case = jnp.where(t < 3, 0, jnp.where(t == 3, 1, 2))
        outside = jnp.where(group == 0, WINDOW - t * TILE, 0)

        def attend(whole):
            q = q_all[here, :]
            nt = (((1,), (1,)), ((), ()))
            skip = 0 if whole else TILE
            near = rows(t * TILE + skip, BAND - skip)
            scores = lax.dot_general(q, kv[0, near, :], nt, preferred_element_type=jnp.float32)
            s_far = lax.dot_general(q, far[0], nt, preferred_element_type=jnp.float32) + bias[case]
            col = lax.broadcasted_iota(jnp.int32, (TILE, TILE), 1)
            row = lax.broadcasted_iota(jnp.int32, (TILE, TILE), 0)
            s_mid = scores[:, TILE - skip : WINDOW - skip]
            s_new = jnp.where(col <= row, scores[:, WINDOW - skip :], LOW)
            if whole:
                s_old = jnp.where(col > row, scores[:, :TILE], LOW)
                parts = [s_old, s_mid, s_new, s_far]
            else:
                place = lax.broadcasted_iota(jnp.int32, (1, WINDOW - TILE), 1) + TILE
                parts = [s_mid + jnp.where(place >= outside, 0.0, LOW), s_new, s_far]
            top = functools.reduce(jnp.maximum, [jnp.max(part, axis=1, keepdims=True) for part in parts])
            weights = [jnp.exp2((part - top) * EXP_SCALE) for part in parts]
            total = sum(jnp.sum(part, axis=1, keepdims=True) for part in weights)
            rounded = [part.astype(jnp.bfloat16) for part in weights]
            mixed = jnp.dot(
                jnp.concatenate(rounded[:-1], axis=1), kv[1, near, :], preferred_element_type=jnp.float32
            )
            mixed = mixed + jnp.dot(rounded[-1], far[1], preferred_element_type=jnp.float32)
            o_all[here, :] = (mixed / total).astype(jnp.bfloat16)

        @pl.when(outside > 0)
        def _():
            attend(False)

        @pl.when(outside <= 0)
        def _():
            attend(True)

        target = out.at[:, cols(h * RING + x)]
        for e in range(2):
            r = 2 * half + lax.rem(h + e, 2)
            result = o_all.at[rows(j * BLK + r * PIECE, PIECE)]

            def send(result=result, r=r):
                pltpu.make_async_remote_copy(
                    src_ref=result,
                    dst_ref=target,
                    send_sem=o_send,
                    recv_sem=o_sem,
                    device_id=(first + j, r),
                    device_id_type=MESH,
                ).start()

            if e:
                send()
            else:
                mine = (dx == 0) & (d == flip)

                @pl.when(mine)
                def _():
                    pltpu.make_async_copy(result, target, o_sem).start()

                pl.when(jnp.logical_not(mine))(send)

        return carry

    lax.fori_loop(0, STEPS, step, 0)

    wait(kv.at[:, pl.ds(0, 3 * BLK)], send_sem.at[0])
    wait(q_all.at[pl.ds(0, 3 * BLK)], send_sem.at[1])
    pl.when(has_next)(functools.partial(wait, kv.at[:, pl.ds(0, WINDOW)], halo_send))
    for d in range(1, GROUPS):
        pl.when(group + d < GROUPS)(functools.partial(wait, far.at[:, pl.ds(d * SUMM, SUMM)], far_send.at[d]))
    wait(o_all.at[pl.ds(0, ROWS - PIECE)], o_send)
    wait(out, o_sem)


def on_device(queries, key_rows, value_rows):
    dma = pltpu.SemaphoreType.DMA
    return pl.pallas_call(
        kernel,
        name="attention",
        out_shape=jax.ShapeDtypeStruct((BLK // HEAD_DEV, HEAD_DEV * RING * HD), jnp.bfloat16),
        in_specs=[pl.BlockSpec(memory_space=pltpu.MemorySpace.HBM)] * 3,
        out_specs=pl.BlockSpec(memory_space=pltpu.VMEM),
        scratch_shapes=[
            pltpu.VMEM((ROWS, HD), jnp.bfloat16),
            pltpu.VMEM((2, WINDOW + ROWS, HD), jnp.bfloat16),
            pltpu.VMEM((2, FAR, HD), jnp.bfloat16),
            pltpu.VMEM((ROWS, HD), jnp.bfloat16),
            pltpu.VMEM((3, TILE, FAR), jnp.float32),
            dma((RING, PARTS)),
            dma((RING, HALF)),
            dma,
            dma((GROUPS,)),
            dma,
            dma((2,)),
            dma,
            dma((GROUPS,)),
            dma,
            pltpu.SemaphoreType.REGULAR,
            pltpu.SemaphoreType.REGULAR,
        ],
        compiler_params=pltpu.CompilerParams(
            collective_id=1, has_side_effects=True, vmem_limit_bytes=VMEM_KIB << 10
        ),
    )(queries, key_rows, value_rows)


def solution(mesh):
    placed = (P("ctx", "head"), P("ctx", "head"), P("ctx", "head"))
    return jax.shard_map(
        on_device, mesh=mesh, in_specs=placed, out_specs=P(("ctx", "head"), None), check_vma=False
    )
```
